32 devices in a mesh: gx: 4 (over z), gy: 2 (over core), gz: 4 (over y, x).
Axes of the slice: x: 2, y: 2, z: 4, core: 2. Of those that a mesh axis runs over, the one named last changes fastest.
Arguments:
- charge: float32 [32, 64, 512], P('gx', 'gy', 'gz'), may hold values from -60 to 60
- texture: float32 [32, 64, 512], P('gx', 'gy', 'gz'), may hold values from 0.5 to 2
- material_eps: float32 [6], replicated, may hold values from 1 to 12
- layer_material: int32 [512], P('gz'), may hold values from 0 to 5
- gate_volts: float32 [1000], replicated, may hold values from -1 to 1
- block_cond: float32 [4096, 128], P(('gx', 'gy', 'gz')), may hold values from 2 to 20
- block_gate: int32 [4096], P(('gx', 'gy', 'gz')), may hold values from 0 to 999
- block_dest: int32 [4096], P(('gx', 'gy', 'gz')), may hold values from 0 to 7, as said below
- block_column: int32 [4096], P(('gx', 'gy', 'gz')), may hold values from 0 to 255
- initial: float32 [32, 64, 512], P('gx', 'gy', 'gz'), may hold values from -2 to 2
Outputs:
- potential: float32 [32, 64, 512], P('gx', 'gy', 'gz')
- residual_norm: float32 [], replicated
The draws below stay inside these ranges and needn't reach their ends.
Inputs may be any that keep to these rules, and one draw needn't show every extreme that they name: `block_dest`: among the blocks of one device no value appears more than 64 times; one value appears exactly 64 times among the blocks of every device.
All inputs are finite; a program needn't handle non-finite values.
Results may differ from the reference program's by a relative error of at most 0.00002.
Values sent between devices are 32-bit elements; how exact they have to be, the bound alone decides.
A program may use at most 64 MiB of HBM per device.

```python
import math
import jax
import jax.numpy as jnp

CX = 8
CY = 32
CZ = 128
SWEEPS = 4
MATERIALS = 6
GATES = 1000
B_DEV = 128
PEERS = 8
CAP = 64
NX = 32
NY = 64
NZ = 512
NBLOCKS = 4096
COLUMNS = 256
N_GY = 2
N_GZ = 4


def draw_block_dest(key, part):
    hot_key, rest_key = jax.random.split(key)
    hot_dest = jax.random.randint(hot_key, (), 0, PEERS)
    sender_keys = jax.random.split(rest_key, NBLOCKS // B_DEV)

    def per_sender(sender_key):
        first_key, second_key = jax.random.split(sender_key)
        slot_ids = jax.random.permutation(first_key, (PEERS - 1) * CAP)[:B_DEV - CAP]
        others = slot_ids // CAP
        others = others + (others >= hot_dest).astype(jnp.int32)
        destinations = jnp.concatenate([jnp.full((CAP,), hot_dest, jnp.int32), others.astype(jnp.int32)])
        return jax.random.permutation(second_key, destinations)
    return jax.vmap(per_sender)(sender_keys).reshape(NBLOCKS).astype(jnp.int32)


def with_ends(values, rng, low, top_value):
    place = [jax.random.randint(jax.random.fold_in(rng, axis), (), 0, length) for axis, length in enumerate(values.shape)]
    widest = values.shape.index(max(values.shape))
    beside = place[:widest] + [(place[widest] + 1) % values.shape[widest]] + place[widest + 1:]
    return values.at[tuple(place)].set(low).at[tuple(beside)].set(top_value)


def block_levels(stream_key, shape, cuts, smallest, largest):
    gain = 1.0
    for position, parts in cuts:
        draws = jax.random.uniform(jax.random.fold_in(jax.random.fold_in(stream_key, 6), position), (parts,), jnp.float32, smallest / len(cuts), largest / len(cuts))
        gain = gain * jnp.repeat(jnp.exp(draws), shape[position] // parts).reshape((-1,) + (1,) * (len(shape) - 1 - position))
    return gain


def normal_values(own_key, extent, spread, limit, cuts=(), kind=jnp.bfloat16):
    gain = block_levels(own_key, extent, cuts, -0.22, 0.18) if cuts else 1.0
    values = jax.random.normal(own_key, extent, jnp.float32) * spread * gain
    return jnp.minimum(jnp.maximum(values, -limit), limit).astype(kind)


def setup_inputs(seed: int = 0) -> dict:
    splits = jax.random.split(jax.random.key(seed), 11)
    return {
        "charge": normal_values(splits[0], (NX, NY, NZ), 10.0, 60.0, ((0, 4), (1, 2), (2, 4)), jnp.float32),
        "texture": jnp.clip(jnp.exp(math.log(2.0) - 1.3862944 * jax.random.uniform(splits[1], (NX, NY, NZ), jnp.float32) ** block_levels(splits[1], (NX, NY, NZ), ((0, 4), (1, 2), (2, 4)), -0.2, 0.2)), 0.5, 2.0),
        "material_eps": jnp.clip(jnp.exp(jax.random.uniform(splits[2], (MATERIALS,), jnp.float32, math.log(1.0), math.log(12.0))), 1.0, 12.0),
        "layer_material": with_ends(jax.random.randint(splits[3], (NZ,), 0, MATERIALS), jax.random.fold_in(splits[3], 1), 0, MATERIALS - 1).astype(jnp.int32),
        "gate_volts": jnp.clip(jax.random.uniform(splits[4], (GATES,), jnp.float32, -1.0, 1.0), -1.0, 1.0),
        "block_cond": jnp.clip(jnp.exp(math.log(20.0) - 2.3025851 * jax.random.uniform(splits[5], (NBLOCKS, CZ), jnp.float32) ** block_levels(splits[5], (NBLOCKS, CZ), ((0, 32),), -0.2, 0.2)), 2.0, 20.0),
        "block_gate": with_ends(jax.random.randint(splits[6], (NBLOCKS,), 0, GATES), jax.random.fold_in(splits[6], 1), 0, GATES - 1).astype(jnp.int32),
        "block_dest": draw_block_dest(jax.random.fold_in(splits[10], 71), 0),
        "block_column": with_ends(jax.random.randint(splits[8], (NBLOCKS,), 0, COLUMNS), jax.random.fold_in(splits[8], 1), 0, COLUMNS - 1).astype(jnp.int32),
        "initial": normal_values(splits[9], (NX, NY, NZ), 0.3, 2.0, ((0, 4), (1, 2), (2, 4)), jnp.float32),
    }


relaxation = 0.8

def shifted(padded):
    return [padded[:-2, 1:-1, 1:-1], padded[2:, 1:-1, 1:-1], padded[1:-1, :-2, 1:-1], padded[1:-1, 2:, 1:-1], padded[1:-1, 1:-1, :-2], padded[1:-1, 1:-1, 2:]]

def face_coefficients(padded):
    centre = padded[1:-1, 1:-1, 1:-1]
    result = []
    for neighbour in shifted(padded):
        result.append(2.0 * centre * neighbour / (centre + neighbour))
    return result

def neighbour_sum(coefficients, padded):
    pieces = shifted(padded)
    total_sum = coefficients[0] * pieces[0]
    for index in range(1, 6):
        total_sum = total_sum + coefficients[index] * pieces[index]
    return total_sum

def reference(charge, texture, material_eps, layer_material, gate_volts, block_cond, block_gate, block_dest, block_column, initial):
    layer_eps = material_eps[layer_material]
    permittivity = texture * layer_eps[None, None, :]
    coefficients = face_coefficients(jnp.pad(permittivity, 1))
    block_volts = gate_volts[block_gate]
    block_source = block_cond * block_volts[:, None]
    numbers = jnp.arange(NBLOCKS, dtype=jnp.int32)
    slab = (numbers // B_DEV % N_GZ).astype(jnp.int32)
    row_x = block_dest // N_GY * CX + block_column // CY
    row_y = block_dest % N_GY * CY + block_column % CY
    column = (row_x * NY + row_y).astype(jnp.int32)
    empty = jnp.zeros((NX * NY, N_GZ, CZ), jnp.float32)
    coupling = empty.at[column, slab].add(block_cond).reshape(NX, NY, NZ)
    injected = empty.at[column, slab].add(block_source).reshape(NX, NY, NZ)
    diagonal_sum = coefficients[0]
    for index in range(1, 6):
        diagonal_sum = diagonal_sum + coefficients[index]
    diagonal_sum = diagonal_sum + coupling
    forcing = charge + injected
    potential = initial
    for sweep in range(SWEEPS):
        neighbours = neighbour_sum(coefficients, jnp.pad(potential, 1))
        potential = (1.0 - relaxation) * potential + relaxation * (forcing + neighbours) / diagonal_sum
    neighbours = neighbour_sum(coefficients, jnp.pad(potential, 1))
    residual = forcing + neighbours - diagonal_sum * potential
    residual_norm = jnp.sqrt(jnp.sum(residual * residual) / (NX * NY * NZ))
    return (potential, residual_norm)
```

```python
import functools

import jax
import jax.numpy as jnp
from jax import lax
from jax.experimental import pallas as pl
from jax.experimental.pallas import tpu as pltpu
from jax.sharding import PartitionSpec as P

SWEEPS = 4
RELAX = 0.8
MESH = pl.DeviceIdType.MESH
F32 = jnp.float32
BF16 = jnp.bfloat16


def each(low, high, body):
    if high - low <= 16:
        for k in range(low, high):
            body(k)
    else:
        def step(k, carry):
            body(k)
            return carry
        lax.fori_loop(low, high, step, 0)


def terms(value):
    high = value.astype(BF16).astype(F32)
    rest = value - high
    mid = rest.astype(BF16).astype(F32)
    return high, mid, rest - mid


def kernel(
    sizes,
    eps_ref,
    charge_ref,
    texture_ref,
    layer_ref,
    volts_ref,
    cond_ref,
    gate_ref,
    dest_ref,
    column_ref,
    initial_ref,
    out_ref,
    norm_ref,
    field,
    coef,
    blocks_out,
    blocks_in,
    face_y,
    face_z,
    halo_x,
    halo_y,
    halo_z,
    coupled,
    part,
    sums,
    part2,
    sums2,
    block_send,
    block_recv,
    face_send,
    face_recv,
    sum_send,
    sum_recv,
    sum2_send,
    sum2_recv,
):
    grid_x, grid_y, grid_z, capacity, used = sizes
    peers = grid_x * grid_y
    cx, cy, cz = charge_ref.shape
    exchanges = SWEEPS + 2
    ix, iy, iz = lax.axis_index("gx"), lax.axis_index("gy"), lax.axis_index("gz")
    me = ix * grid_y + iy
    here = (ix, iy, iz)
    counts = (grid_x, grid_y, grid_z)
    names = ("gx", "gy", "gz")

    def peer(k):
        target = lax.rem(me + k, peers)
        return target, {"gx": target // grid_y, "gy": lax.rem(target, grid_y)}

    def layer(k):
        return {"gz": lax.rem(iz + k, grid_z)}

    def beside(axis, side):
        return here[axis] > 0 if side == 0 else here[axis] < counts[axis] - 1

    for axis, halo in enumerate((halo_x, halo_y, halo_z)):
        for side in range(2):
            @pl.when(jnp.logical_not(beside(axis, side)))
            def _(halo=halo, side=side):
                halo[:, side] = jnp.zeros(halo.shape[:1] + halo.shape[2:], F32)

    barrier = pltpu.get_barrier_semaphore()
    each(1, peers, lambda k: pl.semaphore_signal(barrier, inc=1, device_id=peer(k)[1], device_id_type=MESH))
    each(1, grid_z, lambda k: pl.semaphore_signal(barrier, inc=1, device_id=layer(k), device_id_type=MESH))

    lane = lax.broadcasted_iota(jnp.int32, (cy, cz), 1)

    def pack(exchange, value):
        face_y[exchange, 0] = value[:, 0, :]
        face_y[exchange, 1] = value[:, cy - 1, :]
        faces = jnp.zeros((cy, cz), F32)
        for x in range(cx):
            faces = jnp.where(lane == x, value[x, :, cz - 1:cz], faces)
            faces = jnp.where(lane == cx + x, value[x, :, 0:1], faces)
        face_z[exchange] = faces

    def face_copy(exchange, axis, side):
        step = counts[axis] - 1 if side == 0 else 1
        if axis == 0:
            source, target = field.at[exchange, 0 if side == 0 else cx - 1], halo_x
        elif axis == 1:
            source, target = face_y.at[exchange, side], halo_y
        else:
            source, target = face_z.at[exchange], halo_z
        return pltpu.make_async_remote_copy(
            src_ref=source,
            dst_ref=target.at[exchange, 1 - side],
            send_sem=face_send.at[exchange, 2 * axis + side],
            recv_sem=face_recv.at[exchange, 2 * axis + 1 - side],
            device_id={names[axis]: lax.rem(here[axis] + step, counts[axis])},
            device_id_type=MESH,
        )

    def send_faces(exchange):
        for axis in (2, 0, 1):
            for side in range(2):
                @pl.when(beside(axis, side))
                def _(axis=axis, side=side):
                    face_copy(exchange, axis, side).start()

    def wait_faces(exchange):
        for axis in (1, 0, 2):
            for side in range(2):
                @pl.when(beside(axis, side))
                def _(axis=axis, side=side):
                    face_copy(exchange, axis, 1 - side).wait_recv()

    row_y = lax.broadcasted_iota(jnp.int32, (cx, cy, cz), 1)
    lane3 = lax.broadcasted_iota(jnp.int32, (cx, cy, cz), 2)

    def shifted(exchange, value):
        low_x = jnp.concatenate([halo_x[exchange, 0][None], value[:-1]], axis=0)
        high_x = jnp.concatenate([value[1:], halo_x[exchange, 1][None]], axis=0)
        low_y = jnp.where(row_y == 0, halo_y[exchange, 0][:, None, :], pltpu.roll(value, 1, 1))
        high_y = jnp.where(row_y == cy - 1, halo_y[exchange, 1][:, None, :], pltpu.roll(value, cy - 1, 1))
        low_face, high_face = halo_z[exchange, 0], halo_z[exchange, 1]
        low_z = jnp.stack([jnp.broadcast_to(low_face[:, x:x + 1], (cy, cz)) for x in range(cx)])
        high_z = jnp.stack([jnp.broadcast_to(high_face[:, cx + x:cx + x + 1], (cy, cz)) for x in range(cx)])
        low_z = jnp.where(lane3 == 0, low_z, pltpu.roll(value, 1, 2))
        high_z = jnp.where(lane3 == cz - 1, high_z, pltpu.roll(value, cz - 1, 2))
        return low_x, high_x, low_y, high_y, low_z, high_z

    layers = layer_ref[...]
    layer_eps = jnp.zeros(layers.shape, F32)
    for m in range(eps_ref.shape[0]):
        layer_eps = jnp.where(layers == m, eps_ref[m], layer_eps)
    permittivity = texture_ref[...] * layer_eps[None]
    field[0] = permittivity
    pack(0, permittivity)
    initial = initial_ref[...]
    field[1] = initial
    pack(1, initial)

    count = cond_ref.shape[0]
    down = lax.broadcasted_iota(jnp.int32, (count, count), 0)
    across = lax.broadcasted_iota(jnp.int32, (count, count), 1)

    def upright(row):
        return jnp.sum(jnp.where(down == across, row, jnp.zeros_like(row)), axis=1, keepdims=True)

    dest_row = dest_ref[...].astype(F32)
    dest_col = upright(dest_row)
    same = dest_row == dest_col
    rank_row = jnp.sum(jnp.where(same & (down < across), 1.0, 0.0), axis=0, keepdims=True)
    position_row = dest_row * capacity + rank_row
    position_col = upright(position_row)
    gate_col = upright(gate_ref[...].astype(F32)).astype(jnp.int32)
    gates = volts_ref.shape[1]
    gate_ids = lax.broadcasted_iota(jnp.int32, (count, gates), 1)
    volts_col = jnp.sum(jnp.where(gate_ids == gate_col, volts_ref[...], 0.0), axis=1, keepdims=True)
    column_col = upright(column_ref[...].astype(F32))

    slots = peers * capacity
    slot = lax.broadcasted_iota(jnp.int32, (slots, count), 0)
    chosen = jnp.where(slot == position_row.astype(jnp.int32), 1.0, 0.0).astype(BF16)
    high, mid, low = terms(cond_ref[...])
    pair = jnp.concatenate([high, mid], axis=1).astype(BF16)
    moved = jnp.dot(chosen, pair, preferred_element_type=F32)
    moved_low = jnp.dot(chosen, low.astype(BF16), preferred_element_type=F32)
    moved = moved[:, :cz] + moved[:, cz:] + moved_low
    blocks_out[:, :capacity, :] = moved.reshape(peers, capacity, cz)
    place = lax.rem(across, capacity)
    position_int = position_col.astype(jnp.int32)

    def details(p):
        mine = position_int == place + p * capacity
        blocks_out[p, capacity:capacity + 1, :] = jnp.sum(jnp.where(mine, column_col, 0.0), axis=0, keepdims=True)
        blocks_out[p, capacity + 1:capacity + 2, :] = jnp.sum(jnp.where(mine, volts_col, 0.0), axis=0, keepdims=True)

    blocks_out[:, capacity + 2:, :] = jnp.zeros((peers, 6, cz), F32)
    each(0, peers, details)

    pl.semaphore_wait(barrier, peers - 1 + grid_z - 1)

    def block_copy(k):
        target, device = peer(k)
        return pltpu.make_async_remote_copy(
            src_ref=blocks_out.at[target],
            dst_ref=blocks_in.at[k],
            send_sem=block_send.at[k],
            recv_sem=block_recv.at[k],
            device_id=device,
            device_id_type=MESH,
        )

    send_faces(0)
    send_faces(1)
    each(1, peers, lambda k: block_copy(k).start())

    columns = cx * cy
    depth = -(-3 * capacity // cz) * cz
    column_ids = lax.broadcasted_iota(jnp.int32, (columns, cz), 0)
    eye = lax.broadcasted_iota(jnp.int32, (capacity, cz), 0) == lax.broadcasted_iota(jnp.int32, (capacity, cz), 1)

    def product(blocks):
        cond = blocks[:capacity]
        row = blocks[capacity:capacity + 1].astype(jnp.int32)
        volts = jnp.sum(jnp.where(eye, blocks[capacity + 1:capacity + 2], 0.0), axis=1, keepdims=True)
        both = jnp.concatenate([cond, cond * volts], axis=1)
        pieces = list(terms(both))
        if depth > 3 * capacity:
            pieces.append(jnp.zeros((depth - 3 * capacity, 2 * cz), F32))
        right = jnp.concatenate(pieces, axis=0).astype(BF16)
        hit = jnp.where(column_ids == row, 1.0, 0.0).astype(BF16)
        left = jnp.concatenate([hit] * (depth // cz), axis=1)
        return jnp.dot(left, right, preferred_element_type=F32)

    coupled[...] = product(blocks_out[me])

    wait_faces(0)
    coefficients = []
    for neighbour in shifted(0, permittivity):
        coefficients.append(2.0 * permittivity * neighbour / (permittivity + neighbour))
    diagonal = coefficients[0]
    for index in range(1, 6):
        diagonal = diagonal + coefficients[index]
    for index in range(6):
        coef[index] = coefficients[index]
    wait_faces(1)

    def neighbours(exchange, value):
        pieces = shifted(exchange, value)
        total = coef[0] * pieces[0]
        for index in range(1, 6):
            total = total + coef[index] * pieces[index]
        return total

    first = neighbours(1, initial_ref[...]) + charge_ref[...]
    coef[6] = first
    coef[7] = diagonal

    def arrive(k):
        block_copy(k).wait_recv()
        coupled[...] += product(blocks_in[k])

    each(1, peers, arrive)
    diagonal = coef[7] + coupled[:, :cz].reshape(cx, cy, cz)
    injected = coupled[:, cz:].reshape(cx, cy, cz)
    scale = RELAX / diagonal
    potential = (1.0 - RELAX) * initial_ref[...] + scale * (coef[6] + injected)
    field[2] = potential
    pack(2, potential)
    send_faces(2)
    for index in range(6):
        coef[index] = coef[index] * scale
    forcing = (charge_ref[...] + injected) * scale
    coef[6] = forcing
    coef[7] = diagonal * (1.0 / RELAX)

    for exchange in range(2, exchanges - 1):
        wait_faces(exchange)
        potential = field[exchange]
        potential = (1.0 - RELAX) * potential + (coef[6] + neighbours(exchange, potential))
        field[exchange + 1] = potential
        pack(exchange + 1, potential)
        send_faces(exchange + 1)

    last = exchanges - 1
    out_ref[...] = field[last]
    wait_faces(last)
    potential = field[last]
    residual = (coef[6] + neighbours(last, potential) - RELAX * potential) * coef[7]
    squares = jnp.sum(residual * residual, axis=0)
    total = squares[:8]
    for y in range(8, cy, 8):
        total = total + squares[y:y + 8]

    part[...] = total
    sums[me] = total

    def sum_copy(k):
        return pltpu.make_async_remote_copy(
            src_ref=part,
            dst_ref=sums.at[me],
            send_sem=sum_send.at[k],
            recv_sem=sum_recv.at[k],
            device_id=peer(k)[1],
            device_id_type=MESH,
        )

    def sum2_copy(k):
        return pltpu.make_async_remote_copy(
            src_ref=part2,
            dst_ref=sums2.at[iz],
            send_sem=sum2_send.at[k],
            recv_sem=sum2_recv.at[k],
            device_id=layer(k),
            device_id_type=MESH,
        )

    each(1, peers, lambda k: sum_copy(k).start())
    each(1, peers, lambda k: sum_copy(k).wait_recv())
    total = jnp.sum(sums[...], axis=0)
    part2[...] = total
    sums2[iz] = total
    each(1, grid_z, lambda k: sum2_copy(k).start())
    each(1, peers, lambda k: block_copy(k).wait_send())
    for exchange in range(exchanges):
        for axis in range(3):
            for side in range(2):
                @pl.when(beside(axis, side))
                def _(exchange=exchange, axis=axis, side=side):
                    face_copy(exchange, axis, side).wait_send()
    each(1, peers, lambda k: sum_copy(k).wait_send())
    each(1, grid_z, lambda k: sum2_copy(k).wait_recv())
    total = jnp.sum(sums2[...], axis=0)
    cells = cx * cy * cz * grid_x * grid_y * grid_z
    norm_ref[...] = jnp.sqrt(jnp.sum(total, keepdims=True) / cells)
    each(1, grid_z, lambda k: sum2_copy(k).wait_send())


def on_device(
    sizes,
    charge,
    texture,
    material_eps,
    layer_material,
    gate_volts,
    block_cond,
    block_gate,
    block_dest,
    block_column,
    initial,
):
    grid_x, grid_y, grid_z, capacity, _ = sizes
    peers = grid_x * grid_y
    cx, cy, cz = charge.shape
    exchanges = SWEEPS + 2
    vmem = pl.BlockSpec(memory_space=pltpu.VMEM)
    dma = pltpu.SemaphoreType.DMA
    potential, norm = pl.pallas_call(
        functools.partial(kernel, sizes),
        out_shape=(jax.ShapeDtypeStruct(charge.shape, F32), jax.ShapeDtypeStruct((1, 1), F32)),
        in_specs=[pl.BlockSpec(memory_space=pltpu.SMEM)] + [vmem] * 9,
        out_specs=(vmem, vmem),
        scratch_shapes=[
            pltpu.VMEM((exchanges, cx, cy, cz), F32),
            pltpu.VMEM((8, cx, cy, cz), F32),
            pltpu.VMEM((peers, capacity + 8, cz), F32),
            pltpu.VMEM((peers, capacity + 8, cz), F32),
            pltpu.VMEM((exchanges, 2, cx, cz), F32),
            pltpu.VMEM((exchanges, cy, cz), F32),
            pltpu.VMEM((exchanges, 2, cy, cz), F32),
            pltpu.VMEM((exchanges, 2, cx, cz), F32),
            pltpu.VMEM((exchanges, 2, cy, cz), F32),
            pltpu.VMEM((cx * cy, 2 * cz), F32),
            pltpu.VMEM((8, cz), F32),
            pltpu.VMEM((peers, 8, cz), F32),
            pltpu.VMEM((8, cz), F32),
            pltpu.VMEM((grid_z, 8, cz), F32),
            dma((peers,)),
            dma((peers,)),
            dma((exchanges, 6)),
            dma((exchanges, 6)),
            dma((peers,)),
            dma((peers,)),
            dma((grid_z,)),
            dma((grid_z,)),
        ],
        compiler_params=pltpu.CompilerParams(
            collective_id=0, has_side_effects=True, vmem_limit_bytes=32 * 1024 * 1024
        ),
    )(
        material_eps,
        charge,
        texture,
        layer_material[None, :],
        gate_volts[None, :],
        block_cond,
        block_gate[None, :],
        block_dest[None, :],
        block_column[None, :],
        initial,
    )
    return potential, norm[0, 0]


def solution(mesh):
    grid_x, grid_y, grid_z = mesh.shape["gx"], mesh.shape["gy"], mesh.shape["gz"]
    peers = grid_x * grid_y

    def program(*arrays):
        count = arrays[5].shape[0] // (peers * grid_z)
        used = max(2, 4 * count // peers)
        capacity = -(-used // 8) * 8
        sizes = (grid_x, grid_y, grid_z, capacity, used)
        in_specs = (
            P("gx", "gy", "gz"),
            P("gx", "gy", "gz"),
            P(),
            P("gz"),
            P(),
            P(("gx", "gy", "gz"), None),
            P(("gx", "gy", "gz")),
            P(("gx", "gy", "gz")),
            P(("gx", "gy", "gz")),
            P("gx", "gy", "gz"),
        )
        return jax.shard_map(
            functools.partial(on_device, sizes),
            mesh=mesh,
            in_specs=in_specs,
            out_specs=(P("gx", "gy", "gz"), P()),
            check_vma=False,
        )(*arrays)

    return program
```

```python
import functools

import jax
import jax.numpy as jnp
from jax import lax
from jax.experimental import pallas as pl
from jax.experimental.pallas import tpu as pltpu
from jax.sharding import PartitionSpec as P

SWEEPS = 4
RELAX = 0.8
MESH = pl.DeviceIdType.MESH
F32 = jnp.float32
BF16 = jnp.bfloat16


def each(low, high, body):
    if high - low <= 32:
        for k in range(low, high):
            body(k)
    else:
        def step(k, carry):
            body(k)
            return carry
        lax.fori_loop(low, high, step, 0)


def middle_first(count, body):
    half = count // 2
    if count > 16:
        each(1, count, body)
        return
    for k in sorted(range(1, count), key=lambda k: abs(k - half)):
        body(k)


def terms(value):
    high = value.astype(BF16).astype(F32)
    rest = value - high
    mid = rest.astype(BF16).astype(F32)
    return high, mid, rest - mid


def kernel(
    sizes,
    eps_in,
    charge_in,
    texture_in,
    layer_in,
    volts_in,
    cond_in,
    gate_in,
    dest_in,
    column_in,
    initial_in,
    out_ref,
    norm_ref,
    eps_ref,
    charge_ref,
    texture_ref,
    layer_ref,
    volts_ref,
    cond_ref,
    gate_ref,
    dest_ref,
    column_ref,
    load_sem,
    rims,
    faces_of,
    field,
    coef,
    blocks_out,
    blocks_in,
    face_y,
    face_z,
    halo_x,
    halo_y,
    halo_z,
    coupled,
    part,
    sums,
    block_send,
    block_recv,
    face_send,
    face_recv,
    sum_send,
    sum_recv,
):
    grid_x, grid_y, grid_z, capacity, used = sizes
    peers = grid_x * grid_y
    cx, cy, cz = charge_ref.shape
    exchanges = SWEEPS + 2
    ix, iy, iz = lax.axis_index("gx"), lax.axis_index("gy"), lax.axis_index("gz")
    me = ix * grid_y + iy
    here = (ix, iy, iz)
    counts = (grid_x, grid_y, grid_z)
    names = ("gx", "gy", "gz")

    def peer(k):
        target = lax.rem(me + k, peers)
        return target, {"gx": target // grid_y, "gy": lax.rem(target, grid_y)}

    devices = peers * grid_z
    number = me * grid_z + iz

    def anyone(k):
        target = lax.rem(number + k, devices)
        slab = target // grid_z
        return {"gx": slab // grid_y, "gy": lax.rem(slab, grid_y), "gz": lax.rem(target, grid_z)}

    def beside(axis, side):
        return here[axis] > 0 if side == 0 else here[axis] < counts[axis] - 1

    for axis, halo in enumerate((halo_x, halo_y, halo_z)):
        for side in range(2):
            @pl.when(jnp.logical_not(beside(axis, side)))
            def _(halo=halo, side=side):
                halo[:, side] = jnp.zeros(halo.shape[:1] + halo.shape[2:], F32)

    barrier = pltpu.get_barrier_semaphore()
    each(1, devices, lambda k: pl.semaphore_signal(barrier, inc=1, device_id=anyone(k), device_id_type=MESH))

    pairs = (
        (dest_in, dest_ref),
        (column_in, column_ref),
        (gate_in, gate_ref),
        (volts_in, volts_ref),
        (cond_in, cond_ref),
        (eps_in, eps_ref),
        (layer_in, layer_ref),
        (texture_in, texture_ref),
        (initial_in, field.at[1]),
        (charge_in, charge_ref),
    )
    loads = [pltpu.make_async_copy(a, b, load_sem.at[i]) for i, (a, b) in enumerate(pairs)]
    for load in loads:
        load.start()

    lane = lax.broadcasted_iota(jnp.int32, (cy, cz), 1)

    def pack(exchange, value):
        face_y[exchange, 0] = value[:, 0, :]
        face_y[exchange, 1] = value[:, cy - 1, :]
        faces = jnp.zeros((cy, cz), F32)
        for x in range(cx):
            faces = jnp.where(lane == x, value[x, :, cz - 1:cz], faces)
            faces = jnp.where(lane == cx + x, value[x, :, 0:1], faces)
        face_z[exchange] = faces

    def face_copy(exchange, axis, side):
        step = counts[axis] - 1 if side == 0 else 1
        if axis == 0:
            source, target = field.at[exchange, 0 if side == 0 else cx - 1], halo_x
        elif axis == 1:
            source, target = face_y.at[exchange, side], halo_y
        else:
            source, target = face_z.at[exchange], halo_z
        return pltpu.make_async_remote_copy(
            src_ref=source,
            dst_ref=target.at[exchange, 1 - side],
            send_sem=face_send.at[exchange, 2 * axis + side],
            recv_sem=face_recv.at[exchange, 2 * axis + 1 - side],
            device_id={names[axis]: lax.rem(here[axis] + step, counts[axis])},
            device_id_type=MESH,
        )

    def send_faces(exchange):
        for axis in (2, 0, 1):
            for side in range(2):
                @pl.when(beside(axis, side))
                def _(axis=axis, side=side):
                    face_copy(exchange, axis, side).start()

    def wait_faces(exchange):
        for axis in (1, 0, 2):
            for side in range(2):
                @pl.when(beside(axis, side))
                def _(axis=axis, side=side):
                    face_copy(exchange, axis, 1 - side).wait_recv()

    row_y = lax.broadcasted_iota(jnp.int32, (cx, cy, cz), 1)
    lane3 = lax.broadcasted_iota(jnp.int32, (cx, cy, cz), 2)

    def shifted(exchange, value):
        low_x = jnp.concatenate([halo_x[exchange, 0][None], value[:-1]], axis=0)
        high_x = jnp.concatenate([value[1:], halo_x[exchange, 1][None]], axis=0)
        low_y = jnp.where(row_y == 0, halo_y[exchange, 0][:, None, :], pltpu.roll(value, 1, 1))
        high_y = jnp.where(row_y == cy - 1, halo_y[exchange, 1][:, None, :], pltpu.roll(value, cy - 1, 1))
        low_face, high_face = halo_z[exchange, 0], halo_z[exchange, 1]
        low_z = jnp.stack([jnp.broadcast_to(low_face[:, x:x + 1], (cy, cz)) for x in range(cx)])
        high_z = jnp.stack([jnp.broadcast_to(high_face[:, cx + x:cx + x + 1], (cy, cz)) for x in range(cx)])
        low_z = jnp.where(lane3 == 0, low_z, pltpu.roll(value, 1, 2))
        high_z = jnp.where(lane3 == cz - 1, high_z, pltpu.roll(value, cz - 1, 2))
        return low_x, high_x, low_y, high_y, low_z, high_z

    for load in loads[:5]:
        load.wait()
    count = cond_ref.shape[0]
    down = lax.broadcasted_iota(jnp.int32, (count, count), 0)
    across = lax.broadcasted_iota(jnp.int32, (count, count), 1)

    def upright(row):
        return jnp.sum(jnp.where(down == across, row, jnp.zeros_like(row)), axis=1, keepdims=True)

    dest_row = dest_ref[...].astype(F32)
    dest_col = upright(dest_row)
    same = dest_row == dest_col
    rank_row = jnp.sum(jnp.where(same & (down < across), 1.0, 0.0), axis=0, keepdims=True)
    position_row = dest_row * capacity + rank_row
    position_col = upright(position_row)
    gate_col = upright(gate_ref[...].astype(F32)).astype(jnp.int32)
    gates = volts_ref.shape[1]
    gate_ids = lax.broadcasted_iota(jnp.int32, (count, gates), 1)
    volts_col = jnp.sum(jnp.where(gate_ids == gate_col, volts_ref[...], 0.0), axis=1, keepdims=True)
    column_col = upright(column_ref[...].astype(F32))

    slots = peers * capacity
    slot = lax.broadcasted_iota(jnp.int32, (slots, count), 0)
    chosen = jnp.where(slot == position_row.astype(jnp.int32), 1.0, 0.0).astype(BF16)
    high, mid, low = terms(cond_ref[...])
    pair = jnp.concatenate([high, mid], axis=1).astype(BF16)
    moved = jnp.dot(chosen, pair, preferred_element_type=F32)
    moved_low = jnp.dot(chosen, low.astype(BF16), preferred_element_type=F32)
    moved = moved[:, :cz] + moved[:, cz:] + moved_low
    blocks_out[:, :capacity, :] = moved.reshape(peers, capacity, cz)
    place = lax.rem(across, capacity)
    position_int = position_col.astype(jnp.int32)

    def details(p):
        mine = position_int == place + p * capacity
        blocks_out[p, capacity:capacity + 1, :] = jnp.sum(jnp.where(mine, column_col, 0.0), axis=0, keepdims=True)
        blocks_out[p, capacity + 1:capacity + 2, :] = jnp.sum(jnp.where(mine, volts_col, 0.0), axis=0, keepdims=True)

    blocks_out[:, capacity + 2:, :] = jnp.zeros((peers, 6, cz), F32)
    each(0, peers, details)

    for load in loads[5:9]:
        load.wait()
    layers = layer_ref[...]
    layer_eps = jnp.zeros(layers.shape, F32)
    for m in range(eps_ref.shape[1]):
        layer_eps = jnp.where(layers == m, eps_ref[:, m:m + 1], layer_eps)
    permittivity = texture_ref[...] * layer_eps[None]
    field[0] = permittivity
    pack(0, permittivity)
    pack(1, field[1])

    pl.semaphore_wait(barrier, devices - 1)

    def block_copy(k):
        target, device = peer(k)
        return pltpu.make_async_remote_copy(
            src_ref=blocks_out.at[target],
            dst_ref=blocks_in.at[k],
            send_sem=block_send.at[k],
            recv_sem=block_recv.at[k],
            device_id=device,
            device_id_type=MESH,
        )

    send_faces(0)
    send_faces(1)
    middle_first(peers, lambda k: block_copy(k).start())

    columns = cx * cy
    depth = -(-3 * capacity // cz) * cz
    column_ids = lax.broadcasted_iota(jnp.int32, (columns, cz), 0)
    eye = lax.broadcasted_iota(jnp.int32, (capacity, cz), 0) == lax.broadcasted_iota(jnp.int32, (capacity, cz), 1)

    def product(blocks):
        cond = blocks[:capacity]
        row = blocks[capacity:capacity + 1].astype(jnp.int32)
        volts = jnp.sum(jnp.where(eye, blocks[capacity + 1:capacity + 2], 0.0), axis=1, keepdims=True)
        both = jnp.concatenate([cond, cond * volts], axis=1)
        pieces = list(terms(both))
        if depth > 3 * capacity:
            pieces.append(jnp.zeros((depth - 3 * capacity, 2 * cz), F32))
        right = jnp.concatenate(pieces, axis=0).astype(BF16)
        hit = jnp.where(column_ids == row, 1.0, 0.0).astype(BF16)
        left = jnp.concatenate([hit] * (depth // cz), axis=1)
        return jnp.dot(left, right, preferred_element_type=F32)

    coupled[...] = product(blocks_out[me])

    wait_faces(0)
    coefficients = []
    for neighbour in shifted(0, permittivity):
        coefficients.append(2.0 * permittivity * neighbour / (permittivity + neighbour))
    diagonal = coefficients[0]
    for index in range(1, 6):
        diagonal = diagonal + coefficients[index]
    for index in range(6):
        coef[index] = coefficients[index]
    wait_faces(1)

    def neighbours(exchange, value):
        pieces = shifted(exchange, value)
        total = coef[0] * pieces[0]
        for index in range(1, 6):
            total = total + coef[index] * pieces[index]
        return total

    loads[9].wait()
    first = neighbours(1, field[1]) + charge_ref[...]
    coef[6] = first
    coef[7] = diagonal

    def arrive(k):
        block_copy(k).wait_recv()
        coupled[...] += product(blocks_in[k])

    middle_first(peers, arrive)
    diagonal = coef[7] + coupled[:, :cz].reshape(cx, cy, cz)
    injected = coupled[:, cz:].reshape(cx, cy, cz)
    scale = RELAX / diagonal
    potential = (1.0 - RELAX) * field[1] + scale * (coef[6] + injected)
    field[2] = potential
    pack(2, potential)
    send_faces(2)
    scaled = [coef[index] * scale for index in range(6)]
    coef[0] = scaled[0]
    coef[1] = scaled[1]
    coef[2] = jnp.where(row_y == 0, 0.0, scaled[2])
    coef[3] = jnp.where(row_y == cy - 1, 0.0, scaled[3])
    coef[4] = jnp.where(lane3 == 0, 0.0, scaled[4])
    coef[5] = jnp.where(lane3 == cz - 1, 0.0, scaled[5])
    faces_of[0] = scaled[2][:, 0, :]
    faces_of[1] = scaled[3][:, cy - 1, :]
    coef[8] = jnp.where(lane3 == 0, scaled[4], jnp.where(lane3 == cz - 1, scaled[5], 0.0))
    coef[6] = (charge_ref[...] + injected) * scale
    coef[7] = diagonal * (1.0 / RELAX)

    def inner(exchange):
        value = field[exchange]
        blank = jnp.zeros((1, cy, cz), F32)
        total = coef[6] + coef[0] * jnp.concatenate([blank, value[:-1]], axis=0)
        total = total + coef[1] * jnp.concatenate([value[1:], blank], axis=0)
        total = total + coef[2] * pltpu.roll(value, 1, 1)
        total = total + coef[3] * pltpu.roll(value, cy - 1, 1)
        total = total + coef[4] * pltpu.roll(value, 1, 2)
        return total + coef[5] * pltpu.roll(value, cz - 1, 2)

    def outer(exchange):
        rims[0] += coef[0, 0] * halo_x[exchange, 0]
        rims[cx - 1] += coef[1, cx - 1] * halo_x[exchange, 1]
        low_y = (faces_of[0] * halo_y[exchange, 0])[:, None, :]
        high_y = (faces_of[1] * halo_y[exchange, 1])[:, None, :]
        low_face, high_face = halo_z[exchange, 0], halo_z[exchange, 1]
        near = []
        for x in range(cx):
            near.append(jnp.where(lane < cz // 2, low_face[:, x:x + 1], high_face[:, cx + x:cx + x + 1]))
        total = rims[...] + jnp.where(row_y == 0, low_y, 0.0) + jnp.where(row_y == cy - 1, high_y, 0.0)
        return total + coef[8] * jnp.stack(near)

    for exchange in range(2, exchanges - 1):
        rims[...] = inner(exchange) + (1.0 - RELAX) * field[exchange]
        wait_faces(exchange)
        potential = outer(exchange)
        field[exchange + 1] = potential
        pack(exchange + 1, potential)
        send_faces(exchange + 1)

    last = exchanges - 1
    store = pltpu.make_async_copy(field.at[last], out_ref, load_sem.at[0])
    store.start()
    rims[...] = inner(last) - RELAX * field[last]
    wait_faces(last)
    residual = outer(last) * coef[7]
    squares = jnp.sum(residual * residual, axis=0)
    total = squares[:8]
    for y in range(8, cy, 8):
        total = total + squares[y:y + 8]

    total = jnp.sum(total, axis=0, keepdims=True)
    part[...] = total
    sums[number] = total

    def sum_copy(k):
        return pltpu.make_async_remote_copy(
            src_ref=part,
            dst_ref=sums.at[number],
            send_sem=sum_send.at[k],
            recv_sem=sum_recv.at[k],
            device_id=anyone(k),
            device_id_type=MESH,
        )

    each(1, devices, lambda k: sum_copy(k).start())
    each(1, peers, lambda k: block_copy(k).wait_send())
    for exchange in range(exchanges):
        for axis in range(3):
            for side in range(2):
                @pl.when(beside(axis, side))
                def _(exchange=exchange, axis=axis, side=side):
                    face_copy(exchange, axis, side).wait_send()
    each(1, devices, lambda k: sum_copy(k).wait_send())
    each(1, devices, lambda k: sum_copy(k).wait_recv())
    total = jnp.sum(sums[...], axis=0)
    cells = cx * cy * cz * devices
    store.wait()
    norm_ref[...] = jnp.sqrt(jnp.sum(total, keepdims=True) / cells)


def on_device(
    sizes,
    charge,
    texture,
    material_eps,
    layer_material,
    gate_volts,
    block_cond,
    block_gate,
    block_dest,
    block_column,
    initial,
):
    grid_x, grid_y, grid_z, capacity, _ = sizes
    peers = grid_x * grid_y
    cx, cy, cz = charge.shape
    exchanges = SWEEPS + 2
    vmem = pl.BlockSpec(memory_space=pltpu.VMEM)
    dma = pltpu.SemaphoreType.DMA
    potential, norm = pl.pallas_call(
        functools.partial(kernel, sizes),
        out_shape=(jax.ShapeDtypeStruct(charge.shape, F32), jax.ShapeDtypeStruct((1, 1), F32)),
        in_specs=[pl.BlockSpec(memory_space=pltpu.HBM)] * 10,
        out_specs=(pl.BlockSpec(memory_space=pltpu.HBM), vmem),
        scratch_shapes=[
            pltpu.VMEM((1, material_eps.shape[0]), F32),
            pltpu.VMEM((cx, cy, cz), F32),
            pltpu.VMEM((cx, cy, cz), F32),
            pltpu.VMEM((1, cz), jnp.int32),
            pltpu.VMEM((1, gate_volts.shape[0]), F32),
            pltpu.VMEM(block_cond.shape, F32),
            pltpu.VMEM((1, block_gate.shape[0]), jnp.int32),
            pltpu.VMEM((1, block_dest.shape[0]), jnp.int32),
            pltpu.VMEM((1, block_column.shape[0]), jnp.int32),
            dma((10,)),
            pltpu.VMEM((cx, cy, cz), F32),
            pltpu.VMEM((2, cx, cz), F32),
            pltpu.VMEM((exchanges, cx, cy, cz), F32),
            pltpu.VMEM((9, cx, cy, cz), F32),
            pltpu.VMEM((peers, capacity + 8, cz), F32),
            pltpu.VMEM((peers, capacity + 8, cz), F32),
            pltpu.VMEM((exchanges, 2, cx, cz), F32),
            pltpu.VMEM((exchanges, cy, cz), F32),
            pltpu.VMEM((exchanges, 2, cy, cz), F32),
            pltpu.VMEM((exchanges, 2, cx, cz), F32),
            pltpu.VMEM((exchanges, 2, cy, cz), F32),
            pltpu.VMEM((cx * cy, 2 * cz), F32),
            pltpu.VMEM((1, cz), F32),
            pltpu.VMEM((peers * grid_z, 1, cz), F32),
            dma((peers,)),
            dma((peers,)),
            dma((exchanges, 6)),
            dma((exchanges, 6)),
            dma((peers * grid_z,)),
            dma((peers * grid_z,)),
        ],
        compiler_params=pltpu.CompilerParams(
            collective_id=0, has_side_effects=True, vmem_limit_bytes=60 * 1024 * 1024
        ),
    )(
        material_eps[None, :],
        charge,
        texture,
        layer_material[None, :],
        gate_volts[None, :],
        block_cond,
        block_gate[None, :],
        block_dest[None, :],
        block_column[None, :],
        initial,
    )
    return potential, norm[0, 0]


def solution(mesh):
    grid_x, grid_y, grid_z = mesh.shape["gx"], mesh.shape["gy"], mesh.shape["gz"]
    peers = grid_x * grid_y

    def program(*arrays):
        count = arrays[5].shape[0] // (peers * grid_z)
        used = max(2, 4 * count // peers)
        capacity = -(-used // 8) * 8
        sizes = (grid_x, grid_y, grid_z, capacity, used)
        in_specs = (
            P("gx", "gy", "gz"),
            P("gx", "gy", "gz"),
            P(),
            P("gz"),
            P(),
            P(("gx", "gy", "gz"), None),
            P(("gx", "gy", "gz")),
            P(("gx", "gy", "gz")),
            P(("gx", "gy", "gz")),
            P("gx", "gy", "gz"),
        )
        return jax.shard_map(
            functools.partial(on_device, sizes),
            mesh=mesh,
            in_specs=in_specs,
            out_specs=(P("gx", "gy", "gz"), P()),
            check_vma=False,
        )(*arrays)

    return program
```

```python
import functools

import jax
import jax.numpy as jnp
from jax import lax
from jax.experimental import pallas as pl
from jax.experimental.pallas import tpu as pltpu
from jax.sharding import PartitionSpec as P

SWEEPS = 4
RELAX = 0.8
MESH = pl.DeviceIdType.MESH
F32 = jnp.float32
BF16 = jnp.bfloat16


def each(low, high, body):
    if high - low <= 32:
        for k in range(low, high):
            body(k)
    else:
        def step(k, carry):
            body(k)
            return carry
        lax.fori_loop(low, high, step, 0)


def middle_first(count, body):
    half = count // 2
    if count > 32:
        each(1, count, body)
        return
    for k in sorted(range(1, count), key=lambda k: abs(k - half)):
        body(k)


def terms(value):
    high = value.astype(BF16).astype(F32)
    rest = value - high
    mid = rest.astype(BF16).astype(F32)
    return high, mid, rest - mid


def kernel(
    sizes,
    eps_in,
    charge_in,
    texture_in,
    layer_in,
    volts_in,
    cond_in,
    gate_in,
    dest_in,
    column_in,
    initial_in,
    out_ref,
    norm_ref,
    eps_ref,
    charge_ref,
    texture_ref,
    layer_ref,
    volts_ref,
    cond_ref,
    gate_ref,
    dest_ref,
    column_ref,
    load_sem,
    rims,
    faces_of,
    field,
    coef,
    blocks_out,
    blocks_in,
    face_y,
    face_z,
    halo_x,
    halo_y,
    halo_z,
    coupled,
    part,
    sums,
    block_send,
    block_recv,
    face_send,
    face_recv,
    sum_send,
    sum_recv,
):
    grid_x, grid_y, grid_z, capacity, used = sizes
    peers = grid_x * grid_y
    cx, cy, cz = charge_ref.shape
    exchanges = SWEEPS + 2
    ix, iy, iz = lax.axis_index("gx"), lax.axis_index("gy"), lax.axis_index("gz")
    me = ix * grid_y + iy
    here = (ix, iy, iz)
    counts = (grid_x, grid_y, grid_z)
    names = ("gx", "gy", "gz")

    def peer(k):
        target = lax.rem(me + k, peers)
        return target, {"gx": target // grid_y, "gy": lax.rem(target, grid_y)}

    devices = peers * grid_z
    number = me * grid_z + iz

    def anyone(k):
        target = lax.rem(number + k, devices)
        slab = target // grid_z
        return {"gx": slab // grid_y, "gy": lax.rem(slab, grid_y), "gz": lax.rem(target, grid_z)}

    def beside(axis, side):
        return here[axis] > 0 if side == 0 else here[axis] < counts[axis] - 1

    for axis, halo in enumerate((halo_x, halo_y, halo_z)):
        for side in range(2):
            @pl.when(jnp.logical_not(beside(axis, side)))
            def _(halo=halo, side=side):
                halo[:, side] = jnp.zeros(halo.shape[:1] + halo.shape[2:], F32)

    barrier = pltpu.get_barrier_semaphore()
    each(1, devices, lambda k: pl.semaphore_signal(barrier, inc=1, device_id=anyone(k), device_id_type=MESH))

    pairs = (
        (dest_in, dest_ref),
        (column_in, column_ref),
        (gate_in, gate_ref),
        (volts_in, volts_ref),
        (cond_in, cond_ref),
        (eps_in, eps_ref),
        (layer_in, layer_ref),
        (texture_in, texture_ref),
        (initial_in, field.at[1]),
        (charge_in, charge_ref),
    )
    loads = [pltpu.make_async_copy(a, b, load_sem.at[i]) for i, (a, b) in enumerate(pairs)]
    for load in loads:
        load.start()

    lane8 = lax.broadcasted_iota(jnp.int32, (8, cz), 1)
    half = cx * cy // 8

    def spread(face, x, start):
        tiles = []
        for b in range(cy // 8):
            j = start + x + cx * b
            tiles.append(jnp.broadcast_to(face[:, j:j + 1], (8, cz)))
        return jnp.concatenate(tiles, axis=0)

    def pack(exchange, value):
        face_y[exchange, 0] = value[:, 0, :]
        face_y[exchange, 1] = value[:, cy - 1, :]
        top = jnp.zeros((8, cz), F32)
        bottom = jnp.zeros((8, cz), F32)
        for x in range(cx):
            for b in range(cy // 8):
                rows = value[x, 8 * b:8 * b + 8]
                top = jnp.where(lane8 == x + cx * b, rows[:, cz - 1:cz], top)
                bottom = jnp.where(lane8 == half + x + cx * b, rows[:, 0:1], bottom)
        face_z[exchange] = jnp.where(lane8 < half, top, bottom)

    def face_copy(exchange, axis, side):
        step = counts[axis] - 1 if side == 0 else 1
        at = pl.ds(0, 2) if exchange == 0 else exchange
        if axis == 0:
            source, target = field.at[at, 0 if side == 0 else cx - 1], halo_x
        elif axis == 1:
            source, target = face_y.at[at, side], halo_y
        else:
            source, target = face_z.at[at], halo_z
        return pltpu.make_async_remote_copy(
            src_ref=source,
            dst_ref=target.at[at, 1 - side],
            send_sem=face_send.at[exchange, 2 * axis + side],
            recv_sem=face_recv.at[exchange, 2 * axis + 1 - side],
            device_id={names[axis]: lax.rem(here[axis] + step, counts[axis])},
            device_id_type=MESH,
        )

    def send_faces(exchange):
        for axis in (2, 0, 1):
            for side in range(2):
                @pl.when(beside(axis, side))
                def _(axis=axis, side=side):
                    face_copy(exchange, axis, side).start()

    def wait_faces(exchange):
        for axis in (1, 0, 2):
            for side in range(2):
                @pl.when(beside(axis, side))
                def _(axis=axis, side=side):
                    face_copy(exchange, axis, 1 - side).wait_recv()

    row_y = lax.broadcasted_iota(jnp.int32, (cx, cy, cz), 1)
    lane3 = lax.broadcasted_iota(jnp.int32, (cx, cy, cz), 2)

    def shifted(exchange, value):
        low_x = jnp.concatenate([halo_x[exchange, 0][None], value[:-1]], axis=0)
        high_x = jnp.concatenate([value[1:], halo_x[exchange, 1][None]], axis=0)
        low_y = jnp.where(row_y == 0, halo_y[exchange, 0][:, None, :], pltpu.roll(value, 1, 1))
        high_y = jnp.where(row_y == cy - 1, halo_y[exchange, 1][:, None, :], pltpu.roll(value, cy - 1, 1))
        low_face, high_face = halo_z[exchange, 0], halo_z[exchange, 1]
        low_z = jnp.stack([spread(low_face, x, 0) for x in range(cx)])
        high_z = jnp.stack([spread(high_face, x, half) for x in range(cx)])
        low_z = jnp.where(lane3 == 0, low_z, pltpu.roll(value, 1, 2))
        high_z = jnp.where(lane3 == cz - 1, high_z, pltpu.roll(value, cz - 1, 2))
        return low_x, high_x, low_y, high_y, low_z, high_z

    for load in loads[:5]:
        load.wait()
    count = cond_ref.shape[0]
    down = lax.broadcasted_iota(jnp.int32, (count, count), 0)
    across = lax.broadcasted_iota(jnp.int32, (count, count), 1)

    def upright(row):
        return jnp.sum(jnp.where(down == across, row, jnp.zeros_like(row)), axis=1, keepdims=True)

    dest_row = dest_ref[...].astype(F32)
    dest_col = upright(dest_row)
    same = dest_row == dest_col
    rank_row = jnp.sum(jnp.where(same & (down < across), 1.0, 0.0), axis=0, keepdims=True)
    position_row = dest_row * capacity + rank_row
    position_col = upright(position_row)
    gate_col = upright(gate_ref[...].astype(F32)).astype(jnp.int32)
    gates = volts_ref.shape[1]
    gate_ids = lax.broadcasted_iota(jnp.int32, (count, gates), 1)
    volts_col = jnp.sum(jnp.where(gate_ids == gate_col, volts_ref[...], 0.0), axis=1, keepdims=True)
    column_col = upright(column_ref[...].astype(F32))

    slots = peers * capacity
    slot = lax.broadcasted_iota(jnp.int32, (slots, count), 0)
    chosen = jnp.where(slot == position_row.astype(jnp.int32), 1.0, 0.0).astype(BF16)
    high, mid, low = terms(cond_ref[...])
    pair = jnp.concatenate([high, mid], axis=1).astype(BF16)
    moved = jnp.dot(chosen, pair, preferred_element_type=F32)
    moved_low = jnp.dot(chosen, low.astype(BF16), preferred_element_type=F32)
    moved = moved[:, :cz] + moved[:, cz:] + moved_low
    blocks_out[:, :capacity, :] = moved.reshape(peers, capacity, cz)
    place = lax.rem(across, capacity)
    position_int = position_col.astype(jnp.int32)

    def details(p):
        mine = position_int == place + p * capacity
        blocks_out[p, capacity:capacity + 1, :] = jnp.sum(jnp.where(mine, column_col, 0.0), axis=0, keepdims=True)
        blocks_out[p, capacity + 1:capacity + 2, :] = jnp.sum(jnp.where(mine, volts_col, 0.0), axis=0, keepdims=True)

    blocks_out[:, capacity + 2:, :] = jnp.zeros((peers, 6, cz), F32)
    each(0, peers, details)

    for load in loads[5:9]:
        load.wait()
    layers = layer_ref[...]
    layer_eps = jnp.zeros(layers.shape, F32)
    for m in range(eps_ref.shape[1]):
        layer_eps = jnp.where(layers == m, eps_ref[:, m:m + 1], layer_eps)
    permittivity = texture_ref[...] * layer_eps[None]
    field[0] = permittivity
    pack(0, permittivity)
    pack(1, field[1])

    pl.semaphore_wait(barrier, devices - 1)

    def block_copy(k):
        target, device = peer(k)
        return pltpu.make_async_remote_copy(
            src_ref=blocks_out.at[target],
            dst_ref=blocks_in.at[k],
            send_sem=block_send.at[k],
            recv_sem=block_recv.at[k],
            device_id=device,
            device_id_type=MESH,
        )

    send_faces(0)
    middle_first(peers, lambda k: block_copy(k).start())

    columns = cx * cy
    depth = -(-3 * capacity // cz) * cz
    column_ids = lax.broadcasted_iota(jnp.int32, (columns, cz), 0)
    eye = lax.broadcasted_iota(jnp.int32, (capacity, cz), 0) == lax.broadcasted_iota(jnp.int32, (capacity, cz), 1)

    def product(blocks):
        cond = blocks[:capacity]
        row = blocks[capacity:capacity + 1].astype(jnp.int32)
        volts = jnp.sum(jnp.where(eye, blocks[capacity + 1:capacity + 2], 0.0), axis=1, keepdims=True)
        both = jnp.concatenate([cond, cond * volts], axis=1)
        pieces = list(terms(both))
        if depth > 3 * capacity:
            pieces.append(jnp.zeros((depth - 3 * capacity, 2 * cz), F32))
        right = jnp.concatenate(pieces, axis=0).astype(BF16)
        hit = jnp.where(column_ids == row, 1.0, 0.0).astype(BF16)
        left = jnp.concatenate([hit] * (depth // cz), axis=1)
        return jnp.dot(left, right, preferred_element_type=F32)

    coupled[...] = product(blocks_out[me])

    wait_faces(0)
    coefficients = []
    for neighbour in shifted(0, permittivity):
        coefficients.append(2.0 * permittivity * neighbour / (permittivity + neighbour))
    diagonal = coefficients[0]
    for index in range(1, 6):
        diagonal = diagonal + coefficients[index]
    for index in range(6):
        coef[index] = coefficients[index]

    def neighbours(exchange, value):
        pieces = shifted(exchange, value)
        total = coef[0] * pieces[0]
        for index in range(1, 6):
            total = total + coef[index] * pieces[index]
        return total

    loads[9].wait()
    first = neighbours(1, field[1]) + charge_ref[...]
    coef[6] = first
    coef[7] = diagonal

    def arrive(k):
        block_copy(k).wait_recv()
        coupled[...] += product(blocks_in[k])

    middle_first(peers, arrive)
    diagonal = coef[7] + coupled[:, :cz].reshape(cx, cy, cz)
    injected = coupled[:, cz:].reshape(cx, cy, cz)
    scale = RELAX / diagonal
    potential = (1.0 - RELAX) * field[1] + scale * (coef[6] + injected)
    field[2] = potential
    pack(2, potential)
    send_faces(2)
    scaled = [coef[index] * scale for index in range(6)]
    coef[0] = scaled[0]
    coef[1] = scaled[1]
    coef[2] = jnp.where(row_y == 0, 0.0, scaled[2])
    coef[3] = jnp.where(row_y == cy - 1, 0.0, scaled[3])
    coef[4] = jnp.where(lane3 == 0, 0.0, scaled[4])
    coef[5] = jnp.where(lane3 == cz - 1, 0.0, scaled[5])
    faces_of[0] = scaled[2][:, 0, :]
    faces_of[1] = scaled[3][:, cy - 1, :]
    coef[8] = jnp.where(lane3 == 0, scaled[4], jnp.where(lane3 == cz - 1, scaled[5], 0.0))
    coef[6] = (charge_ref[...] + injected) * scale
    coef[7] = diagonal * (1.0 / RELAX)

    def inner(exchange):
        value = field[exchange]
        blank = jnp.zeros((1, cy, cz), F32)
        total = coef[6] + coef[0] * jnp.concatenate([blank, value[:-1]], axis=0)
        total = total + coef[1] * jnp.concatenate([value[1:], blank], axis=0)
        total = total + coef[2] * pltpu.roll(value, 1, 1)
        total = total + coef[3] * pltpu.roll(value, cy - 1, 1)
        total = total + coef[4] * pltpu.roll(value, 1, 2)
        return total + coef[5] * pltpu.roll(value, cz - 1, 2)

    def outer(exchange):
        rims[0] += coef[0, 0] * halo_x[exchange, 0]
        rims[cx - 1] += coef[1, cx - 1] * halo_x[exchange, 1]
        low_y = (faces_of[0] * halo_y[exchange, 0])[:, None, :]
        high_y = (faces_of[1] * halo_y[exchange, 1])[:, None, :]
        low_face, high_face = halo_z[exchange, 0], halo_z[exchange, 1]
        near = []
        for x in range(cx):
            near.append(jnp.where(lane3[0] < cz // 2, spread(low_face, x, 0), spread(high_face, x, half)))
        total = rims[...] + jnp.where(row_y == 0, low_y, 0.0) + jnp.where(row_y == cy - 1, high_y, 0.0)
        return total + coef[8] * jnp.stack(near)

    for exchange in range(2, exchanges - 1):
        rims[...] = inner(exchange) + (1.0 - RELAX) * field[exchange]
        wait_faces(exchange)
        potential = outer(exchange)
        field[exchange + 1] = potential
        pack(exchange + 1, potential)
        send_faces(exchange + 1)

    last = exchanges - 1
    store = pltpu.make_async_copy(field.at[last], out_ref, load_sem.at[0])
    store.start()
    rims[...] = inner(last) - RELAX * field[last]
    wait_faces(last)
    residual = outer(last) * coef[7]
    squares = jnp.sum(residual * residual, axis=0)
    total = squares[:8]
    for y in range(8, cy, 8):
        total = total + squares[y:y + 8]

    total = jnp.sum(total, axis=0, keepdims=True)
    part[...] = total
    sums[number] = total

    def sum_copy(k):
        return pltpu.make_async_remote_copy(
            src_ref=part,
            dst_ref=sums.at[number],
            send_sem=sum_send.at[k],
            recv_sem=sum_recv.at[k],
            device_id=anyone(k),
            device_id_type=MESH,
        )

    middle_first(devices, lambda k: sum_copy(k).start())
    each(1, peers, lambda k: block_copy(k).wait_send())
    for exchange in (0, *range(2, exchanges)):
        for axis in range(3):
            for side in range(2):
                @pl.when(beside(axis, side))
                def _(exchange=exchange, axis=axis, side=side):
                    face_copy(exchange, axis, side).wait_send()
    each(1, devices, lambda k: sum_copy(k).wait_send())
    each(1, devices, lambda k: sum_copy(k).wait_recv())
    total = jnp.sum(sums[...], axis=0)
    cells = cx * cy * cz * devices
    store.wait()
    norm_ref[...] = jnp.sqrt(jnp.sum(total, keepdims=True) / cells)


def on_device(
    sizes,
    charge,
    texture,
    material_eps,
    layer_material,
    gate_volts,
    block_cond,
    block_gate,
    block_dest,
    block_column,
    initial,
):
    grid_x, grid_y, grid_z, capacity, _ = sizes
    peers = grid_x * grid_y
    cx, cy, cz = charge.shape
    exchanges = SWEEPS + 2
    vmem = pl.BlockSpec(memory_space=pltpu.VMEM)
    dma = pltpu.SemaphoreType.DMA
    potential, norm = pl.pallas_call(
        functools.partial(kernel, sizes),
        out_shape=(jax.ShapeDtypeStruct(charge.shape, F32), jax.ShapeDtypeStruct((1, 1), F32)),
        in_specs=[pl.BlockSpec(memory_space=pltpu.HBM)] * 10,
        out_specs=(pl.BlockSpec(memory_space=pltpu.HBM), vmem),
        scratch_shapes=[
            pltpu.VMEM((1, material_eps.shape[0]), F32),
            pltpu.VMEM((cx, cy, cz), F32),
            pltpu.VMEM((cx, cy, cz), F32),
            pltpu.VMEM((1, cz), jnp.int32),
            pltpu.VMEM((1, gate_volts.shape[0]), F32),
            pltpu.VMEM(block_cond.shape, F32),
            pltpu.VMEM((1, block_gate.shape[0]), jnp.int32),
            pltpu.VMEM((1, block_dest.shape[0]), jnp.int32),
            pltpu.VMEM((1, block_column.shape[0]), jnp.int32),
            dma((10,)),
            pltpu.VMEM((cx, cy, cz), F32),
            pltpu.VMEM((2, cx, cz), F32),
            pltpu.VMEM((exchanges, cx, cy, cz), F32),
            pltpu.VMEM((9, cx, cy, cz), F32),
            pltpu.VMEM((peers, capacity + 8, cz), F32),
            pltpu.VMEM((peers, capacity + 8, cz), F32),
            pltpu.VMEM((exchanges, 2, cx, cz), F32),
            pltpu.VMEM((exchanges, 8, cz), F32),
            pltpu.VMEM((exchanges, 2, cy, cz), F32),
            pltpu.VMEM((exchanges, 2, cx, cz), F32),
            pltpu.VMEM((exchanges, 2, 8, cz), F32),
            pltpu.VMEM((cx * cy, 2 * cz), F32),
            pltpu.VMEM((1, cz), F32),
            pltpu.VMEM((peers * grid_z, 1, cz), F32),
            dma((peers,)),
            dma((peers,)),
            dma((exchanges, 6)),
            dma((exchanges, 6)),
            dma((peers * grid_z,)),
            dma((peers * grid_z,)),
        ],
        compiler_params=pltpu.CompilerParams(
            collective_id=0, has_side_effects=True, vmem_limit_bytes=60 * 1024 * 1024
        ),
    )(
        material_eps[None, :],
        charge,
        texture,
        layer_material[None, :],
        gate_volts[None, :],
        block_cond,
        block_gate[None, :],
        block_dest[None, :],
        block_column[None, :],
        initial,
    )
    return potential, norm[0, 0]


def solution(mesh):
    grid_x, grid_y, grid_z = mesh.shape["gx"], mesh.shape["gy"], mesh.shape["gz"]
    peers = grid_x * grid_y

    def program(*arrays):
        count = arrays[5].shape[0] // (peers * grid_z)
        used = max(2, 4 * count // peers)
        capacity = -(-used // 8) * 8
        sizes = (grid_x, grid_y, grid_z, capacity, used)
        in_specs = (
            P("gx", "gy", "gz"),
            P("gx", "gy", "gz"),
            P(),
            P("gz"),
            P(),
            P(("gx", "gy", "gz"), None),
            P(("gx", "gy", "gz")),
            P(("gx", "gy", "gz")),
            P(("gx", "gy", "gz")),
            P("gx", "gy", "gz"),
        )
        return jax.shard_map(
            functools.partial(on_device, sizes),
            mesh=mesh,
            in_specs=in_specs,
            out_specs=(P("gx", "gy", "gz"), P()),
            check_vma=False,
        )(*arrays)

    return program
```
